32 devices in a mesh: dp: 8 (over z, y), fsdp: 4 (over x, core).
Axes of the slice: x: 2, y: 2, z: 4, core: 2. Of those that a mesh axis runs over, the one named last changes fastest.
Arguments:
- inputs: float32 [640, 8192], P('fsdp', 'dp'), may hold values from -26 to 26, as said below
- norm_gain: float32 [640], P('fsdp'), may hold values from 0.1 to 1.9
- norm_bias: float32 [640], P('fsdp'), may hold values from -3 to 3
- conv_weight: float32 [9, 640, 640], P(None, 'fsdp'), may hold values from -0.078125 to 0.078125
- moment_one: float32 [9, 640, 640], P(None, 'fsdp'), may hold values from -3 to 3
- moment_two: float32 [9, 640, 640], P(None, 'fsdp'), may hold values from 0.5 to 4
- out_grad: float32 [640, 8192], P('fsdp', 'dp'), may hold values from -6 to 6
Outputs:
- block_out: float32 [640, 8192], P('fsdp', 'dp')
- input_grad: float32 [640, 8192], P('fsdp', 'dp')
- new_weight: float32 [9, 640, 640], P(None, 'fsdp')
- new_moment_one: float32 [9, 640, 640], P(None, 'fsdp')
- new_moment_two: float32 [9, 640, 640], P(None, 'fsdp')
The draws below stay inside these ranges and needn't reach their ends.
Inputs may be any that keep to these rules, and one draw needn't show every extreme that they name: `inputs`: activations of mixed channel and pixel scales.
All inputs are finite; a program needn't handle non-finite values.
Results may differ from the reference program's by a relative error of at most 0.0027.
Values may be sent and summed in bfloat16 or wider, within the bound.
A program may use at most 64 MiB of HBM per device.

```python
import math
import jax
import jax.numpy as jnp
from jax import lax

CHANNELS = 640
GROUP_CH = 40
SIDE = 32
IMG_GRP = 1
PIXELS = 8192
N_DP = 8


def draw_inputs(key, part):
    key_scale, key_pixel, key_base, key_offset = jax.random.split(key, 4)
    chan_scale = jnp.exp(jax.random.uniform(key_scale, (CHANNELS, 1), jnp.float32, math.log(0.3), math.log(3.0)))
    pixel_scale = jnp.exp(jax.random.uniform(key_pixel, (1, PIXELS), jnp.float32, math.log(0.5), math.log(2.0)))
    base = jnp.clip(jax.random.normal(key_base, (CHANNELS, PIXELS), jnp.float32), -4.0, 4.0)
    offset = jnp.clip(0.5 * jax.random.normal(key_offset, (CHANNELS, 1), jnp.float32), -1.5, 1.5)
    return (base * chan_scale * pixel_scale + offset).astype(jnp.float32)


def level_of(key, shape, pieces, smallest, top_value):
    gain = 1.0
    for axis_at, parts in pieces:
        heights = jax.random.uniform(jax.random.fold_in(jax.random.fold_in(key, 6), axis_at), (parts,), jnp.float32, smallest / len(pieces), top_value / len(pieces))
        gain = gain * jnp.repeat(jnp.exp(heights), shape[axis_at] // parts).reshape((-1,) + (1,) * (len(shape) - 1 - axis_at))
    return gain


def gaussian(own_key, extent, spread, reach, shards=(), kind=jnp.bfloat16):
    values = jax.random.normal(own_key, extent, jnp.float32) * spread
    if len(shards) > 0:
        values = level_of(own_key, extent, shards, -0.22, 0.18) * values
    return jnp.clip(values, min=-reach, max=reach).astype(kind)


def setup_inputs(seed: int = 0) -> dict:
    seeds = jax.random.split(jax.random.key(seed), 8)
    return {
        "inputs": draw_inputs(jax.random.fold_in(seeds[7], 71), 0),
        "norm_gain": jnp.clip(1.0 + 0.18 * jax.random.normal(seeds[1], (CHANNELS,), jnp.float32), 0.1, 1.9),
        "norm_bias": gaussian(seeds[2], (CHANNELS,), 0.5, 3.0, ((0, 4),), jnp.float32),
        "conv_weight": gaussian(seeds[3], (9, CHANNELS, CHANNELS), (9 * CHANNELS) ** -0.5, 0.078125, ((1, 4),), jnp.float32),
        "moment_one": gaussian(seeds[4], (9, CHANNELS, CHANNELS), 0.5, 3.0, ((1, 4),), jnp.float32),
        "moment_two": jnp.clip(jnp.exp(math.log(4.0) - 2.0794415 * jax.random.uniform(seeds[5], (9, CHANNELS, CHANNELS), jnp.float32) ** level_of(seeds[5], (9, CHANNELS, CHANNELS), ((1, 4),), -0.2, 0.2)), 0.5, 4.0),
        "out_grad": gaussian(seeds[6], (CHANNELS, PIXELS), 1.0, 6.0, ((0, 4), (1, 8)), jnp.float32),
    }


EPS_NORM = 1e-05
BETA_ONE = 0.9
BETA_TWO = 0.999
CORRECT_ONE = 1.0 - 0.9 ** 10
CORRECT_TWO = 1.0 - 0.999 ** 10
LEARN_RATE = 0.001
EPS_ADAM = 1e-08
OFFSETS = ((-1, -1), (-1, 0), (-1, 1), (0, -1), (0, 0), (0, 1), (1, -1), (1, 0), (1, 1))

def shifted(source, row_step, col_step):
    width_all = source.shape[-1]
    position = jnp.arange(width_all, dtype=jnp.int32)
    row_pos = position // SIDE % SIDE
    col_pos = position % SIDE
    inside = (row_pos + row_step >= 0) & (row_pos + row_step < SIDE) & (col_pos + col_step >= 0) & (col_pos + col_step < SIDE)
    margin = SIDE + 1
    padded = jnp.pad(source, ((0, 0), (margin, margin)))
    start_at = margin + row_step * SIDE + col_step
    moved = padded[:, start_at:start_at + width_all]
    return jnp.where(inside[None, :], moved, jnp.zeros_like(moved))

def group_stats(source, norm_gain, norm_bias):
    channels, width_all = source.shape
    images = width_all // (SIDE * SIDE)
    blocks = source.reshape(channels // GROUP_CH, GROUP_CH, images, SIDE * SIDE)
    mean_val = lax.optimization_barrier(jnp.mean(blocks, axis=(1, 3), keepdims=True))
    centred = blocks - mean_val
    var_val = lax.optimization_barrier(jnp.mean(centred * centred, axis=(1, 3), keepdims=True))
    inv_dev = lax.rsqrt(var_val + EPS_NORM)
    normed = (centred * inv_dev).reshape(channels, width_all)
    pre_act = normed * norm_gain[:, None] + norm_bias[:, None]
    return (normed, inv_dev, pre_act)

def group_backward(grad_act, pre_act, normed, inv_dev, norm_gain):
    channels, width_all = grad_act.shape
    images = width_all // (SIDE * SIDE)
    shape_four = (channels // GROUP_CH, GROUP_CH, images, SIDE * SIDE)
    sigmoid_val = jax.nn.sigmoid(pre_act)
    grad_pre = grad_act * sigmoid_val * (1.0 + pre_act * (1.0 - sigmoid_val))
    grad_norm = (grad_pre * norm_gain[:, None]).reshape(shape_four)
    normed_four = normed.reshape(shape_four)
    mean_first = lax.optimization_barrier(jnp.mean(grad_norm, axis=(1, 3), keepdims=True))
    mean_second = lax.optimization_barrier(jnp.mean(grad_norm * normed_four, axis=(1, 3), keepdims=True))
    return (inv_dev * (grad_norm - mean_first - normed_four * mean_second)).reshape(channels, width_all)

def adam_update(conv_weight, moment_one, moment_two, gradient):
    first_new = BETA_ONE * moment_one + (1.0 - BETA_ONE) * gradient
    second_new = BETA_TWO * moment_two + (1.0 - BETA_TWO) * gradient * gradient
    weight_new = conv_weight - LEARN_RATE * (first_new / CORRECT_ONE) / (jnp.sqrt(second_new / CORRECT_TWO) + EPS_ADAM)
    return (weight_new, first_new, second_new)

def reference(inputs, norm_gain, norm_bias, conv_weight, moment_one, moment_two, out_grad):
    weight_half = conv_weight.astype(jnp.bfloat16)
    group_width = IMG_GRP * SIDE * SIDE
    grouped_in = inputs.reshape(CHANNELS, N_DP, group_width).transpose(1, 0, 2)
    grouped_grad = out_grad.reshape(CHANNELS, N_DP, group_width).transpose(1, 0, 2)

    def per_group(grad_total, pair):
        source, upstream = pair
        normed, inv_dev, pre_act = group_stats(source, norm_gain, norm_bias)
        activation = jax.nn.silu(pre_act).astype(jnp.bfloat16)
        grad_half = upstream.astype(jnp.bfloat16)
        conv_out = jnp.zeros(source.shape, jnp.float32)
        grad_act = jnp.zeros(source.shape, jnp.float32)
        grad_taps = []
        for tap_index, (row_step, col_step) in enumerate(OFFSETS):
            moved = shifted(activation, row_step, col_step)
            conv_out = conv_out + jnp.dot(weight_half[tap_index], moved, preferred_element_type=jnp.float32)
            grad_taps.append(lax.dot_general(grad_half, moved, (((1,), (1,)), ((), ())), preferred_element_type=jnp.float32))
            back_term = lax.dot_general(weight_half[tap_index], grad_half, (((0,), (0,)), ((), ())), preferred_element_type=jnp.float32)
            grad_act = grad_act + shifted(back_term, -row_step, -col_step)
        block_out = source + conv_out
        input_grad = upstream + group_backward(grad_act, pre_act, normed, inv_dev, norm_gain)
        return (grad_total + jnp.stack(grad_taps), (block_out, input_grad))
    start_total = jnp.zeros((9, CHANNELS, CHANNELS), jnp.float32)
    grad_total, (outs_grouped, grads_grouped) = lax.scan(per_group, start_total, (grouped_in, grouped_grad))
    block_out = outs_grouped.transpose(1, 0, 2).reshape(CHANNELS, PIXELS)
    input_grad = grads_grouped.transpose(1, 0, 2).reshape(CHANNELS, PIXELS)
    gradient = grad_total / (IMG_GRP * N_DP)
    new_weight, new_moment_one, new_moment_two = adam_update(conv_weight, moment_one, moment_two, gradient)
    return (block_out, input_grad, new_weight, new_moment_one, new_moment_two)
```

```python
import functools

import jax
import jax.numpy as jnp
from jax import lax
from jax.experimental import pallas as pl
from jax.experimental.pallas import tpu as pltpu
from jax.sharding import PartitionSpec as P

GROUP_CH = 40
SIDE = 32


EPS_NORM = 1e-05
BETA_ONE = 0.9
BETA_TWO = 0.999
CORRECT_ONE = 1.0 - 0.9**10
CORRECT_TWO = 1.0 - 0.999**10
LEARN_RATE = 0.001
EPS_ADAM = 1e-08
OFFSETS = ((-1, -1), (-1, 0), (-1, 1), (0, -1), (0, 0), (0, 1), (1, -1), (1, 0), (1, 1))


def shifted(source, row_step, col_step):
    width_all = source.shape[-1]
    position = jnp.arange(width_all, dtype=jnp.int32)
    row_pos = position // SIDE % SIDE
    col_pos = position % SIDE
    inside = (
        (row_pos + row_step >= 0)
        & (row_pos + row_step < SIDE)
        & (col_pos + col_step >= 0)
        & (col_pos + col_step < SIDE)
    )
    margin = SIDE + 1
    padded = jnp.pad(source, ((0, 0), (margin, margin)))
    start_at = margin + row_step * SIDE + col_step
    moved = padded[:, start_at : start_at + width_all]
    return jnp.where(inside[None, :], moved, jnp.zeros_like(moved))


def group_stats(source, norm_gain, norm_bias):
    channels, width_all = source.shape
    images = width_all // (SIDE * SIDE)
    blocks = source.reshape(channels // GROUP_CH, GROUP_CH, images, SIDE * SIDE)
    mean_val = jnp.mean(blocks, axis=(1, 3), keepdims=True)
    centred = blocks - mean_val
    var_val = jnp.mean(centred * centred, axis=(1, 3), keepdims=True)
    inv_dev = lax.rsqrt(var_val + EPS_NORM)
    normed = (centred * inv_dev).reshape(channels, width_all)
    pre_act = normed * norm_gain[:, None] + norm_bias[:, None]
    return (normed, inv_dev, pre_act)


def group_backward(grad_act, pre_act, normed, inv_dev, norm_gain):
    channels, width_all = grad_act.shape
    images = width_all // (SIDE * SIDE)
    shape_four = (channels // GROUP_CH, GROUP_CH, images, SIDE * SIDE)
    sigmoid_val = jax.nn.sigmoid(pre_act)
    grad_pre = grad_act * sigmoid_val * (1.0 + pre_act * (1.0 - sigmoid_val))
    grad_norm = (grad_pre * norm_gain[:, None]).reshape(shape_four)
    normed_four = normed.reshape(shape_four)
    mean_first = jnp.mean(grad_norm, axis=(1, 3), keepdims=True)
    mean_second = jnp.mean(grad_norm * normed_four, axis=(1, 3), keepdims=True)
    return (inv_dev * (grad_norm - mean_first - normed_four * mean_second)).reshape(
        channels, width_all
    )


def body(inputs, norm_gain, norm_bias, conv_weight, moment_one, moment_two, out_grad):
    local_ch, group_width = inputs.shape
    images = group_width // (SIDE * SIDE)
    normed, inv_dev, pre_act = group_stats(inputs, norm_gain, norm_bias)
    activation = jax.nn.silu(pre_act).astype(jnp.bfloat16)
    weight_half = conv_weight.astype(jnp.bfloat16)
    grad_half = out_grad.astype(jnp.bfloat16)
    gathered = lax.all_gather(activation, "fsdp", axis=0, tiled=True)
    conv_out = jnp.zeros((local_ch, group_width), jnp.float32)
    grad_taps = []
    for tap_index, (row_step, col_step) in enumerate(OFFSETS):
        moved = shifted(gathered, row_step, col_step)
        conv_out = conv_out + jnp.dot(
            weight_half[tap_index], moved, preferred_element_type=jnp.float32
        )
        grad_taps.append(
            lax.dot_general(
                grad_half, moved, (((1,), (1,)), ((), ())), preferred_element_type=jnp.float32
            )
        )
    block_out = inputs + conv_out
    summed = lax.psum(jnp.stack(grad_taps), "dp")
    gradient = summed / (images * lax.axis_size("dp"))
    running = jnp.zeros((local_ch * lax.axis_size("fsdp"), group_width), jnp.float32)
    for tap_index, (row_step, col_step) in enumerate(OFFSETS):
        weight_part = weight_half[tap_index]
        back_term = lax.dot_general(
            weight_part, grad_half, (((0,), (0,)), ((), ())), preferred_element_type=jnp.float32
        )
        running = running + shifted(back_term, -row_step, -col_step)
    grad_act = lax.psum_scatter(running, "fsdp", scatter_dimension=0, tiled=True)
    input_grad = out_grad + group_backward(grad_act, pre_act, normed, inv_dev, norm_gain)
    first_new = BETA_ONE * moment_one + (1.0 - BETA_ONE) * gradient
    second_new = BETA_TWO * moment_two + (1.0 - BETA_TWO) * gradient * gradient
    weight_new = conv_weight - LEARN_RATE * (first_new / CORRECT_ONE) / (
        jnp.sqrt(second_new / CORRECT_TWO) + EPS_ADAM
    )
    return (block_out, input_grad, weight_new, first_new, second_new)


CHUNKS = 6
VMEM_STEP = 36 * 1024 * 1024
DP_Y = 2
DP_Z = 4
FSDP = 4
MESH = pl.DeviceIdType.MESH


def tap_mask(row_step, col_step):
    position = lax.broadcasted_iota(jnp.int32, (1, SIDE * SIDE), 1)
    row_pos = position // SIDE + row_step
    col_pos = position % SIDE + col_step
    inside = (row_pos >= 0) & (row_pos < SIDE) & (col_pos >= 0) & (col_pos < SIDE)
    return inside


def lane_shift(value, row_step, col_step):
    step = row_step * SIDE + col_step
    if step == 0:
        return value
    moved = pltpu.roll(value, (-step) % (SIDE * SIDE), 1)
    return jnp.where(tap_mask(row_step, col_step), moved, 0.0)


def step_kernel(
    x_ref,
    gain_ref,
    bias_ref,
    w_ref,
    g_ref,
    block_ref,
    igrad_ref,
    out_ref,
    w_full,
    w_half,
    act,
    shifted_g,
    normed_ref,
    pre_ref,
    back,
    from_sib,
    to_x,
    from_x,
    own_full,
    part,
    from_y,
    half_full,
    half_sum,
    from_z,
    w_sem,
    send_sem,
    recv_sem,
):
    local_ch, width = x_ref.shape
    taps = len(OFFSETS)
    all_rows = part.shape[0]
    chunk = all_rows // CHUNKS
    half = chunk // DP_Y
    shard = half // DP_Z
    dp, fs = lax.axis_index("dp"), lax.axis_index("fsdp")
    pos_z, pos_y = dp // DP_Y, dp % DP_Y
    sib = fs // 2 * 2 + (1 - fs % 2)
    far = (fs + 2) % FSDP
    far_sib = (sib + 2) % FSDP
    sib_id, far_id = (dp, sib), (dp, far)
    y_id = (pos_z * DP_Y + (1 - pos_y), fs)
    z_ids = [((pos_z + d) % DP_Z * DP_Y + pos_y, fs) for d in range(1, DP_Z)]
    next_z = pos_z // 2 * 2 + (1 - pos_z % 2)
    next_id, skip_id = (next_z * DP_Y + pos_y, fs), z_ids[1]

    w_copy = pltpu.make_async_copy(w_ref, w_full, w_sem)
    w_copy.start()
    barrier = pltpu.get_barrier_semaphore()
    peers = [sib_id, far_id, y_id] + z_ids
    for peer in peers:
        pl.semaphore_signal(barrier, inc=1, device_id=peer, device_id_type=MESH)

    def rows_of(index):
        return pl.ds(pl.multiple_of(index * local_ch, local_ch), local_ch)

    def remote(source, target, index, peer):
        return pltpu.make_async_remote_copy(
            src_ref=source,
            dst_ref=target,
            send_sem=send_sem.at[index],
            recv_sem=recv_sem.at[index],
            device_id=peer,
            device_id_type=MESH,
        )

    mine = rows_of(fs)
    inv_devs = []
    count = 1.0 / (GROUP_CH * width)
    pieces = []
    for group in range(local_ch // GROUP_CH):
        rows = slice(group * GROUP_CH, (group + 1) * GROUP_CH)
        value = x_ref[rows, :]
        mean_val = jnp.sum(value) * count
        centred = value - mean_val
        var_val = jnp.sum(centred * centred) * count
        inv_dev = lax.rsqrt(jnp.full((1, 1), var_val + EPS_NORM, jnp.float32))
        inv_devs.append(inv_dev)
        normed = centred * inv_dev
        pre_act = normed * gain_ref[rows, :] + bias_ref[rows, :]
        normed_ref[rows, :] = normed
        pre_ref[rows, :] = pre_act
        pieces.append(pre_act * jax.nn.sigmoid(pre_act))
    act[mine, :] = jnp.concatenate(pieces, axis=0).astype(jnp.bfloat16)

    pl.semaphore_wait(barrier, len(peers))
    act_sib = remote(act.at[mine], act.at[mine], 0, sib_id)
    act_far = remote(act.at[mine], act.at[mine], 1, far_id)
    act_far.start()
    act_sib.start()

    for tap, (row_step, col_step) in enumerate(OFFSETS):
        shifted_g[tap * local_ch : (tap + 1) * local_ch, :] = lane_shift(
            g_ref[...], -row_step, -col_step
        ).astype(jnp.bfloat16)
    spare = all_rows - taps * local_ch
    shifted_g[taps * local_ch :, :] = jnp.zeros((spare, width), jnp.bfloat16)

    w_copy.wait()
    w_half[...] = w_full[...].astype(jnp.bfloat16)

    tile = 512

    def back_tile(step, carry):
        columns = pl.ds(pl.multiple_of(step * tile, tile), tile)
        back[:, columns] = lax.dot_general(
            w_half[...],
            shifted_g[: taps * local_ch, columns],
            (((0,), (0,)), ((), ())),
            preferred_element_type=jnp.float32,
        ).astype(jnp.bfloat16)
        return carry

    lax.fori_loop(0, width // tile, back_tile, 0)
    back_far = remote(back.at[rows_of(far_sib)], from_sib.at[1], 4, sib_id)
    back_own = remote(back.at[rows_of(sib)], from_sib.at[0], 3, sib_id)
    back_far.start()
    back_own.start()

    act_far.wait_recv()
    act_forward = remote(act.at[rows_of(far)], act.at[rows_of(far)], 2, sib_id)
    act_forward.start()
    act_sib.wait_recv()
    act_forward.wait_recv()

    y_copies, z_copies, skip_copies, next_copies, yg_copies = [], [], [], [], []

    def half_rows(step, index):
        return pl.ds(pl.multiple_of(step * chunk + index * half, half), half)

    def partial_sum(step):
        rows = slice(step * chunk, (step + 1) * chunk)
        product = lax.dot_general(
            shifted_g[rows, :],
            act[...],
            (((1,), (1,)), ((), ())),
            preferred_element_type=jnp.float32,
        )
        own_full[rows, :] = product
        part[rows, :] = product.astype(jnp.bfloat16)
        copy = remote(part.at[half_rows(step, 1 - pos_y)], from_y.at[step], 6 + 8 * step, y_id)
        copy.start()
        y_copies.append(copy)

    def place(index_z):
        return index_z % 2 * 2 + index_z // 2

    def shard_rows(index_z):
        return pl.ds(pl.multiple_of(place(index_z) * shard, shard), shard)

    def sum_pair(step):
        y_copies[step].wait_recv()
        total = own_full[half_rows(step, pos_y), :] + from_y[step].astype(jnp.float32)
        half_full[step] = total
        half_sum[step] = total.astype(jnp.bfloat16)
        copies = []
        for d in (2, 1, 3):
            copy = remote(
                half_sum.at[step, shard_rows((pos_z + d) % DP_Z)],
                from_z.at[step, d - 1],
                6 + 8 * step + d,
                z_ids[d - 1],
            )
            copy.start()
            copies.append(copy)
        z_copies.append(copies)

    def sum_line(step):
        for copy in z_copies[step]:
            copy.wait_recv()
        total = half_full[step, shard_rows(pos_z), :]
        for d in range(DP_Z - 1):
            total = total + from_z[step, d].astype(jnp.float32)
        start = step * chunk + pos_y * half + place(pos_z) * shard
        rows = pl.ds(pl.multiple_of(start, shard), shard)
        out_ref[rows, :] = total.astype(jnp.bfloat16)
        copy = remote(out_ref.at[rows], out_ref.at[rows], 6 + 8 * step + 4, skip_id)
        copy.start()
        skip_copies.append(copy)

    def share_pair(step):
        skip_copies[step].wait_recv()
        start = step * chunk + pos_y * half + pos_z % 2 * 2 * shard
        rows = pl.ds(pl.multiple_of(start, 2 * shard), 2 * shard)
        copy = remote(out_ref.at[rows], out_ref.at[rows], 6 + 8 * step + 5, next_id)
        copy.start()
        next_copies.append(copy)

    def share_half(step):
        next_copies[step].wait_recv()
        rows = half_rows(step, pos_y)
        copy = remote(out_ref.at[rows], out_ref.at[rows], 6 + 8 * step + 7, y_id)
        copy.start()
        yg_copies.append(copy)

    def conv_taps(first, last):
        total = x_ref[...] if first == 0 else block_ref[...]
        for tap in range(first, last):
            product = jnp.dot(
                w_half[tap * local_ch : (tap + 1) * local_ch, :],
                act[...],
                preferred_element_type=jnp.float32,
            )
            total = total + lane_shift(product, *OFFSETS[tap])
        block_ref[...] = total

    partial_sum(0)
    partial_sum(1)
    back_far.wait_recv()
    to_x[...] = (
        back[rows_of(far), :].astype(jnp.float32) + from_sib[1].astype(jnp.float32)
    ).astype(jnp.bfloat16)
    back_x = remote(to_x, from_x, 5, far_id)
    back_x.start()
    partial_sum(2)
    sum_pair(0)
    partial_sum(3)
    partial_sum(4)
    sum_pair(1)
    partial_sum(5)
    conv_taps(0, 3)
    sum_line(0)
    sum_pair(2)
    conv_taps(3, 6)
    share_pair(0)
    sum_line(1)
    sum_pair(3)
    conv_taps(6, 9)
    share_half(0)
    share_pair(1)
    sum_line(2)
    sum_pair(4)

    back_own.wait_recv()
    back_x.wait_recv()
    for group in range(local_ch // GROUP_CH):
        rows = slice(group * GROUP_CH, (group + 1) * GROUP_CH)
        grad_act = (
            back[mine, :].astype(jnp.float32)[rows]
            + from_sib[0].astype(jnp.float32)[rows]
            + from_x[...].astype(jnp.float32)[rows]
        )
        pre_act, normed = pre_ref[rows, :], normed_ref[rows, :]
        sigmoid_val = jax.nn.sigmoid(pre_act)
        grad_pre = grad_act * sigmoid_val * (1.0 + pre_act * (1.0 - sigmoid_val))
        grad_norm = grad_pre * gain_ref[rows, :]
        mean_first = jnp.sum(grad_norm) * count
        mean_second = jnp.sum(grad_norm * normed) * count
        igrad_ref[rows, :] = g_ref[rows, :] + inv_devs[group] * (
            grad_norm - mean_first - normed * mean_second
        )

    share_half(1)
    share_pair(2)
    sum_line(3)
    sum_pair(5)
    share_half(2)
    share_pair(3)
    sum_line(4)
    share_half(3)
    share_pair(4)
    sum_line(5)
    share_half(4)
    share_pair(5)
    share_half(5)
    for copy in yg_copies:
        copy.wait_recv()
    for copy in [act_sib, act_far, act_forward, back_far, back_own, back_x]:
        copy.wait_send()
    for copies in z_copies + [skip_copies, next_copies, y_copies, yg_copies]:
        for copy in copies:
            copy.wait_send()


def adam_kernel(scale, sum_ref, w_ref, one_ref, two_ref, w_out, one_out, two_out):
    gradient = sum_ref[...].astype(jnp.float32) * scale
    first_new = BETA_ONE * one_ref[...] + (1.0 - BETA_ONE) * gradient
    second_new = BETA_TWO * two_ref[...] + (1.0 - BETA_TWO) * gradient * gradient
    one_out[...] = first_new
    two_out[...] = second_new
    w_out[...] = w_ref[...] - LEARN_RATE * (first_new / CORRECT_ONE) / (
        jnp.sqrt(second_new / CORRECT_TWO) + EPS_ADAM
    )


def fused_body(inputs, norm_gain, norm_bias, conv_weight, moment_one, moment_two, out_grad):
    local_ch, width = inputs.shape
    taps, _, channels = conv_weight.shape
    unit = 16 * DP_Y * DP_Z * CHUNKS
    all_rows = (taps * local_ch + unit - 1) // unit * unit
    half = all_rows // CHUNKS // DP_Y
    shard = half // DP_Z
    copies = 6 + 8 * CHUNKS
    vmem = pl.BlockSpec(memory_space=pltpu.VMEM)
    flops = 2 * 3 * taps * local_ch * channels * width
    block_out, input_grad, summed = pl.pallas_call(
        step_kernel,
        out_shape=(
            jax.ShapeDtypeStruct(inputs.shape, jnp.float32),
            jax.ShapeDtypeStruct(inputs.shape, jnp.float32),
            jax.ShapeDtypeStruct((all_rows, channels), jnp.bfloat16),
        ),
        in_specs=[vmem, vmem, vmem, pl.BlockSpec(memory_space=pl.ANY), vmem],
        out_specs=(vmem, vmem, vmem),
        scratch_shapes=[
            pltpu.VMEM((taps * local_ch, channels), jnp.float32),
            pltpu.VMEM((taps * local_ch, channels), jnp.bfloat16),
            pltpu.VMEM((channels, width), jnp.bfloat16),
            pltpu.VMEM((all_rows, width), jnp.bfloat16),
            pltpu.VMEM((local_ch, width), jnp.float32),
            pltpu.VMEM((local_ch, width), jnp.float32),
            pltpu.VMEM((channels, width), jnp.bfloat16),
            pltpu.VMEM((2, local_ch, width), jnp.bfloat16),
            pltpu.VMEM((local_ch, width), jnp.bfloat16),
            pltpu.VMEM((local_ch, width), jnp.bfloat16),
            pltpu.VMEM((all_rows, channels), jnp.float32),
            pltpu.VMEM((all_rows, channels), jnp.bfloat16),
            pltpu.VMEM((CHUNKS, half, channels), jnp.bfloat16),
            pltpu.VMEM((CHUNKS, half, channels), jnp.float32),
            pltpu.VMEM((CHUNKS, half, channels), jnp.bfloat16),
            pltpu.VMEM((CHUNKS, DP_Z - 1, shard, channels), jnp.bfloat16),
            pltpu.SemaphoreType.DMA,
            pltpu.SemaphoreType.DMA((copies,)),
            pltpu.SemaphoreType.DMA((copies,)),
        ],
        compiler_params=pltpu.CompilerParams(
            collective_id=0, has_side_effects=True, vmem_limit_bytes=VMEM_STEP
        ),
        cost_estimate=pl.CostEstimate(
            flops=flops, bytes_accessed=8_000_000, transcendentals=4 * local_ch * width
        ),
    )(
        inputs,
        norm_gain[:, None],
        norm_bias[:, None],
        conv_weight.reshape(taps * local_ch, channels),
        out_grad,
    )
    flat = (taps * local_ch, channels)
    scale = 1.0 / (lax.axis_size("dp") * (width // (SIDE * SIDE)))
    block = pl.BlockSpec((local_ch, channels), lambda step: (step, 0))
    updated = pl.pallas_call(
        functools.partial(adam_kernel, scale),
        grid=(taps,),
        out_shape=(jax.ShapeDtypeStruct(flat, jnp.float32),) * 3,
        in_specs=[block] * 4,
        out_specs=(block,) * 3,
        cost_estimate=pl.CostEstimate(
            flops=16 * flat[0] * flat[1],
            bytes_accessed=26 * flat[0] * flat[1],
            transcendentals=2 * flat[0] * flat[1],
        ),
        compiler_params=pltpu.CompilerParams(vmem_limit_bytes=16 * 1024 * 1024),
    )(
        summed,
        conv_weight.reshape(flat),
        moment_one.reshape(flat),
        moment_two.reshape(flat),
    )
    weight_new, first_new, second_new = [leaf.reshape(conv_weight.shape) for leaf in updated]
    return (block_out, input_grad, weight_new, first_new, second_new)


def pick_body(inputs, *rest):
    fits = (
        lax.axis_size("dp") == DP_Y * DP_Z
        and lax.axis_size("fsdp") == FSDP
        and inputs.shape[1] == SIDE * SIDE
        and inputs.shape[0] % 16 == 0
    )
    return (fused_body if fits else body)(inputs, *rest)


def solution(mesh):
    placed = (
        P("fsdp", "dp"),
        P("fsdp"),
        P("fsdp"),
        P(None, "fsdp", None),
        P(None, "fsdp", None),
        P(None, "fsdp", None),
        P("fsdp", "dp"),
    )
    return jax.shard_map(
        pick_body,
        mesh=mesh,
        in_specs=placed,
        out_specs=(
            P("fsdp", "dp"),
            P("fsdp", "dp"),
            P(None, "fsdp", None),
            P(None, "fsdp", None),
            P(None, "fsdp", None),
        ),
        check_vma=False,
    )
```

```python
import functools

import jax
import jax.numpy as jnp
from jax import lax
from jax.experimental import pallas as pl
from jax.experimental.pallas import tpu as pltpu
from jax.sharding import PartitionSpec as P

GROUP_CH = 40
SIDE = 32


EPS_NORM = 1e-05
BETA_ONE = 0.9
BETA_TWO = 0.999
CORRECT_ONE = 1.0 - 0.9**10
CORRECT_TWO = 1.0 - 0.999**10
LEARN_RATE = 0.001
EPS_ADAM = 1e-08
OFFSETS = ((-1, -1), (-1, 0), (-1, 1), (0, -1), (0, 0), (0, 1), (1, -1), (1, 0), (1, 1))


def shifted(source, row_step, col_step):
    width_all = source.shape[-1]
    position = jnp.arange(width_all, dtype=jnp.int32)
    row_pos = position // SIDE % SIDE
    col_pos = position % SIDE
    inside = (
        (row_pos + row_step >= 0)
        & (row_pos + row_step < SIDE)
        & (col_pos + col_step >= 0)
        & (col_pos + col_step < SIDE)
    )
    margin = SIDE + 1
    padded = jnp.pad(source, ((0, 0), (margin, margin)))
    start_at = margin + row_step * SIDE + col_step
    moved = padded[:, start_at : start_at + width_all]
    return jnp.where(inside[None, :], moved, jnp.zeros_like(moved))


def group_stats(source, norm_gain, norm_bias):
    channels, width_all = source.shape
    images = width_all // (SIDE * SIDE)
    blocks = source.reshape(channels // GROUP_CH, GROUP_CH, images, SIDE * SIDE)
    mean_val = jnp.mean(blocks, axis=(1, 3), keepdims=True)
    centred = blocks - mean_val
    var_val = jnp.mean(centred * centred, axis=(1, 3), keepdims=True)
    inv_dev = lax.rsqrt(var_val + EPS_NORM)
    normed = (centred * inv_dev).reshape(channels, width_all)
    pre_act = normed * norm_gain[:, None] + norm_bias[:, None]
    return (normed, inv_dev, pre_act)


def group_backward(grad_act, pre_act, normed, inv_dev, norm_gain):
    channels, width_all = grad_act.shape
    images = width_all // (SIDE * SIDE)
    shape_four = (channels // GROUP_CH, GROUP_CH, images, SIDE * SIDE)
    sigmoid_val = jax.nn.sigmoid(pre_act)
    grad_pre = grad_act * sigmoid_val * (1.0 + pre_act * (1.0 - sigmoid_val))
    grad_norm = (grad_pre * norm_gain[:, None]).reshape(shape_four)
    normed_four = normed.reshape(shape_four)
    mean_first = jnp.mean(grad_norm, axis=(1, 3), keepdims=True)
    mean_second = jnp.mean(grad_norm * normed_four, axis=(1, 3), keepdims=True)
    return (inv_dev * (grad_norm - mean_first - normed_four * mean_second)).reshape(
        channels, width_all
    )


def body(inputs, norm_gain, norm_bias, conv_weight, moment_one, moment_two, out_grad):
    local_ch, group_width = inputs.shape
    images = group_width // (SIDE * SIDE)
    normed, inv_dev, pre_act = group_stats(inputs, norm_gain, norm_bias)
    activation = jax.nn.silu(pre_act).astype(jnp.bfloat16)
    weight_half = conv_weight.astype(jnp.bfloat16)
    grad_half = out_grad.astype(jnp.bfloat16)
    gathered = lax.all_gather(activation, "fsdp", axis=0, tiled=True)
    conv_out = jnp.zeros((local_ch, group_width), jnp.float32)
    grad_taps = []
    for tap_index, (row_step, col_step) in enumerate(OFFSETS):
        moved = shifted(gathered, row_step, col_step)
        conv_out = conv_out + jnp.dot(
            weight_half[tap_index], moved, preferred_element_type=jnp.float32
        )
        grad_taps.append(
            lax.dot_general(
                grad_half, moved, (((1,), (1,)), ((), ())), preferred_element_type=jnp.float32
            )
        )
    block_out = inputs + conv_out
    summed = lax.psum(jnp.stack(grad_taps), "dp")
    gradient = summed / (images * lax.axis_size("dp"))
    running = jnp.zeros((local_ch * lax.axis_size("fsdp"), group_width), jnp.float32)
    for tap_index, (row_step, col_step) in enumerate(OFFSETS):
        weight_part = weight_half[tap_index]
        back_term = lax.dot_general(
            weight_part, grad_half, (((0,), (0,)), ((), ())), preferred_element_type=jnp.float32
        )
        running = running + shifted(back_term, -row_step, -col_step)
    grad_act = lax.psum_scatter(running, "fsdp", scatter_dimension=0, tiled=True)
    input_grad = out_grad + group_backward(grad_act, pre_act, normed, inv_dev, norm_gain)
    first_new = BETA_ONE * moment_one + (1.0 - BETA_ONE) * gradient
    second_new = BETA_TWO * moment_two + (1.0 - BETA_TWO) * gradient * gradient
    weight_new = conv_weight - LEARN_RATE * (first_new / CORRECT_ONE) / (
        jnp.sqrt(second_new / CORRECT_TWO) + EPS_ADAM
    )
    return (block_out, input_grad, weight_new, first_new, second_new)


CHUNKS = 6
VMEM_STEP = 36 * 1024 * 1024
DP_Y = 2
DP_Z = 4
FSDP = 4
MESH = pl.DeviceIdType.MESH


def tap_mask(row_step, col_step):
    position = lax.broadcasted_iota(jnp.int32, (1, SIDE * SIDE), 1)
    row_pos = position // SIDE + row_step
    col_pos = position % SIDE + col_step
    inside = (row_pos >= 0) & (row_pos < SIDE) & (col_pos >= 0) & (col_pos < SIDE)
    return inside


def lane_shift(value, row_step, col_step):
    step = row_step * SIDE + col_step
    if step == 0:
        return value
    moved = pltpu.roll(value, (-step) % (SIDE * SIDE), 1)
    return jnp.where(tap_mask(row_step, col_step), moved, 0.0)


def step_kernel(
    x_hbm,
    affine_ref,
    w_ref,
    g_hbm,
    block_ref,
    igrad_ref,
    out_ref,
    x_ref,
    g_ref,
    w_full,
    w_half,
    act,
    act_next,
    g_half,
    g_next,
    shifted_g,
    shifted_next,
    normed_ref,
    pre_ref,
    back,
    from_sib,
    to_x,
    from_x,
    half_full,
    half_sum,
    from_z,
    load_sem,
    send_sem,
    recv_sem,
):
    local_ch, width = x_ref.shape
    taps = len(OFFSETS)
    all_rows = shifted_g.shape[0]
    chunk = all_rows // CHUNKS
    half = chunk // DP_Y
    shard = half // DP_Z
    dp, fs = lax.axis_index("dp"), lax.axis_index("fsdp")
    pos_z, pos_y = dp // DP_Y, dp % DP_Y
    sib = fs // 2 * 2 + (1 - fs % 2)
    far = (fs + 2) % FSDP
    far_sib = (sib + 2) % FSDP
    sib_id, far_id = (dp, sib), (dp, far)
    y_id = (pos_z * DP_Y + (1 - pos_y), fs)
    z_ids = [((pos_z + d) % DP_Z * DP_Y + pos_y, fs) for d in range(1, DP_Z)]
    next_z = pos_z // 2 * 2 + (1 - pos_z % 2)
    next_id, skip_id = (next_z * DP_Y + pos_y, fs), z_ids[1]

    x_copy = pltpu.make_async_copy(x_hbm, x_ref, load_sem.at[0])
    g_copy = pltpu.make_async_copy(g_hbm, g_ref, load_sem.at[1])
    w_copy = pltpu.make_async_copy(w_ref, w_full, load_sem.at[2])
    x_copy.start()
    g_copy.start()
    w_copy.start()
    barrier = pltpu.get_barrier_semaphore()
    peers = [sib_id, far_id, y_id] + z_ids
    for peer in peers:
        pl.semaphore_signal(barrier, inc=1, device_id=peer, device_id_type=MESH)

    def rows_of(index):
        return pl.ds(pl.multiple_of(index * local_ch, local_ch), local_ch)

    def remote(source, target, index, peer):
        return pltpu.make_async_remote_copy(
            src_ref=source,
            dst_ref=target,
            send_sem=send_sem.at[index],
            recv_sem=recv_sem.at[index],
            device_id=peer,
            device_id_type=MESH,
        )

    mine = rows_of(fs)
    inv_devs = []
    count = 1.0 / (GROUP_CH * width)
    pieces = []
    x_copy.wait()
    for group in range(local_ch // GROUP_CH):
        rows = slice(group * GROUP_CH, (group + 1) * GROUP_CH)
        value = x_ref[rows, :]
        mean_val = jnp.sum(value) * count
        centred = value - mean_val
        var_val = jnp.sum(centred * centred) * count
        inv_dev = lax.rsqrt(jnp.full((1, 1), var_val + EPS_NORM, jnp.float32))
        inv_devs.append(inv_dev)
        normed = centred * inv_dev
        pre_act = normed * affine_ref[rows, 0:1] + affine_ref[rows, 1:2]
        normed_ref[rows, :] = normed
        pre_ref[rows, :] = pre_act
        pieces.append(pre_act * jax.nn.sigmoid(pre_act))
    act[mine, :] = jnp.concatenate(pieces, axis=0).astype(jnp.bfloat16)

    pl.semaphore_wait(barrier, len(peers))
    act_sib = remote(act.at[mine], act.at[mine], 0, sib_id)
    act_far = remote(act.at[mine], act.at[mine], 1, far_id)
    extra = 6 + 8 * CHUNKS
    act_y = remote(act.at[mine], act_next.at[mine], extra, y_id)
    act_y.start()
    act_far.start()
    act_sib.start()
    g_copy.wait()
    g_half[...] = g_ref[...].astype(jnp.bfloat16)
    g_y = remote(g_half, g_next, extra + 1, y_id)
    g_y.start()

    for tap, (row_step, col_step) in enumerate(OFFSETS):
        shifted_g[tap * local_ch : (tap + 1) * local_ch, :] = lane_shift(
            g_ref[...], -row_step, -col_step
        ).astype(jnp.bfloat16)
    spare = all_rows - taps * local_ch
    shifted_g[taps * local_ch :, :] = jnp.zeros((spare, width), jnp.bfloat16)
    shifted_next[taps * local_ch :, :] = jnp.zeros((spare, width), jnp.bfloat16)

    w_copy.wait()
    w_half[...] = w_full[...].astype(jnp.bfloat16)

    tile = 512

    def back_tile(step, carry):
        columns = pl.ds(pl.multiple_of(step * tile, tile), tile)
        back[:, columns] = lax.dot_general(
            w_half[...],
            shifted_g[: taps * local_ch, columns],
            (((0,), (0,)), ((), ())),
            preferred_element_type=jnp.float32,
        ).astype(jnp.bfloat16)
        return carry

    lax.fori_loop(0, width // tile, back_tile, 0)
    back_far = remote(back.at[rows_of(far_sib)], from_sib.at[1], 4, sib_id)
    back_own = remote(back.at[rows_of(sib)], from_sib.at[0], 3, sib_id)
    back_far.start()
    back_own.start()

    act_y.wait_recv()
    next_far = remote(act_next.at[mine], act_next.at[mine], extra + 2, far_id)
    next_sib = remote(act_next.at[mine], act_next.at[mine], extra + 3, sib_id)
    next_far.start()
    next_sib.start()
    act_far.wait_recv()
    act_forward = remote(act.at[rows_of(far)], act.at[rows_of(far)], 2, sib_id)
    act_forward.start()
    act_sib.wait_recv()

    z_copies, skip_copies, next_copies, yg_copies = [], [], [], []

    def half_rows(step, index):
        return pl.ds(pl.multiple_of(step * chunk + index * half, half), half)

    def product(left, right, step):
        return lax.dot_general(
            left[half_rows(step, pos_y), :],
            right[...],
            (((1,), (1,)), ((), ())),
            preferred_element_type=jnp.float32,
        )

    def own_sum(step):
        half_full[step] = product(shifted_g, act, step)

    def place(index_z):
        return index_z % 2 * 2 + index_z // 2

    def shard_rows(index_z):
        return pl.ds(pl.multiple_of(place(index_z) * shard, shard), shard)

    def sum_pair(step):
        total = half_full[step] + product(shifted_next, act_next, step)
        half_full[step] = total
        half_sum[step] = total.astype(jnp.bfloat16)
        copies = []
        for d in (2, 1, 3):
            copy = remote(
                half_sum.at[step, shard_rows((pos_z + d) % DP_Z)],
                from_z.at[step, d - 1],
                6 + 8 * step + d,
                z_ids[d - 1],
            )
            copy.start()
            copies.append(copy)
        z_copies.append(copies)

    def sum_line(step):
        for copy in z_copies[step]:
            copy.wait_recv()
        total = half_full[step, shard_rows(pos_z), :]
        for d in range(DP_Z - 1):
            total = total + from_z[step, d].astype(jnp.float32)
        start = step * chunk + pos_y * half + place(pos_z) * shard
        rows = pl.ds(pl.multiple_of(start, shard), shard)
        out_ref[rows, :] = total.astype(jnp.bfloat16)
        copy = remote(out_ref.at[rows], out_ref.at[rows], 6 + 8 * step + 4, skip_id)
        copy.start()
        skip_copies.append(copy)

    def share_pair(step):
        skip_copies[step].wait_recv()
        start = step * chunk + pos_y * half + pos_z % 2 * 2 * shard
        rows = pl.ds(pl.multiple_of(start, 2 * shard), 2 * shard)
        copy = remote(out_ref.at[rows], out_ref.at[rows], 6 + 8 * step + 5, next_id)
        copy.start()
        next_copies.append(copy)

    def share_half(step):
        next_copies[step].wait_recv()
        rows = half_rows(step, pos_y)
        copy = remote(out_ref.at[rows], out_ref.at[rows], 6 + 8 * step + 7, y_id)
        copy.start()
        yg_copies.append(copy)

    def conv_taps(first, last):
        total = x_ref[...] if first == 0 else block_ref[...]
        for tap in range(first, last):
            product = jnp.dot(
                w_half[tap * local_ch : (tap + 1) * local_ch, :],
                act[...],
                preferred_element_type=jnp.float32,
            )
            total = total + lane_shift(product, *OFFSETS[tap])
        block_ref[...] = total

    back_far.wait_recv()
    to_x[...] = (
        back[rows_of(far), :].astype(jnp.float32) + from_sib[1].astype(jnp.float32)
    ).astype(jnp.bfloat16)
    back_x = remote(to_x, from_x, 5, far_id)
    back_x.start()
    g_y.wait_recv()
    for tap, (row_step, col_step) in enumerate(OFFSETS):
        shifted_next[tap * local_ch : (tap + 1) * local_ch, :] = lane_shift(
            g_next[...].astype(jnp.float32), -row_step, -col_step
        ).astype(jnp.bfloat16)
    act_forward.wait_recv()
    for step in range(CHUNKS):
        own_sum(step)
    next_far.wait_recv()
    next_forward = remote(
        act_next.at[rows_of(far)], act_next.at[rows_of(far)], extra + 4, sib_id
    )
    next_forward.start()
    next_sib.wait_recv()
    next_forward.wait_recv()
    for step in range(CHUNKS):
        sum_pair(step)
        if step >= 4:
            sum_line(step - 4)
    conv_taps(0, 3)
    share_pair(0)
    sum_line(2)
    conv_taps(3, 6)
    share_half(0)
    share_pair(1)
    sum_line(3)
    conv_taps(6, 9)
    share_half(1)
    share_pair(2)
    sum_line(4)

    back_own.wait_recv()
    back_x.wait_recv()
    for group in range(local_ch // GROUP_CH):
        rows = slice(group * GROUP_CH, (group + 1) * GROUP_CH)
        grad_act = (
            back[mine, :].astype(jnp.float32)[rows]
            + from_sib[0].astype(jnp.float32)[rows]
            + from_x[...].astype(jnp.float32)[rows]
        )
        pre_act, normed = pre_ref[rows, :], normed_ref[rows, :]
        sigmoid_val = jax.nn.sigmoid(pre_act)
        grad_pre = grad_act * sigmoid_val * (1.0 + pre_act * (1.0 - sigmoid_val))
        grad_norm = grad_pre * affine_ref[rows, 0:1]
        mean_first = jnp.sum(grad_norm) * count
        mean_second = jnp.sum(grad_norm * normed) * count
        igrad_ref[rows, :] = g_ref[rows, :] + inv_devs[group] * (
            grad_norm - mean_first - normed * mean_second
        )

    share_half(2)
    share_pair(3)
    sum_line(5)
    share_half(3)
    share_pair(4)
    share_half(4)
    share_pair(5)
    share_half(5)
    for copy in yg_copies:
        copy.wait_recv()
    singles = [act_sib, act_far, act_forward, back_far, back_own, back_x]
    for copy in singles + [act_y, g_y, next_far, next_sib, next_forward]:
        copy.wait_send()
    for copies in z_copies + [skip_copies, next_copies, yg_copies]:
        for copy in copies:
            copy.wait_send()


def adam_kernel(scale, sum_ref, w_ref, one_ref, two_ref, w_out, one_out, two_out):
    gradient = sum_ref[...].astype(jnp.float32) * scale
    first_new = BETA_ONE * one_ref[...] + (1.0 - BETA_ONE) * gradient
    second_new = BETA_TWO * two_ref[...] + (1.0 - BETA_TWO) * gradient * gradient
    one_out[...] = first_new
    two_out[...] = second_new
    w_out[...] = w_ref[...] - LEARN_RATE * (first_new / CORRECT_ONE) / (
        jnp.sqrt(second_new / CORRECT_TWO) + EPS_ADAM
    )


def fused_body(inputs, norm_gain, norm_bias, conv_weight, moment_one, moment_two, out_grad):
    local_ch, width = inputs.shape
    taps, _, channels = conv_weight.shape
    unit = 16 * DP_Y * DP_Z * CHUNKS
    all_rows = (taps * local_ch + unit - 1) // unit * unit
    half = all_rows // CHUNKS // DP_Y
    shard = half // DP_Z
    copies = 6 + 8 * CHUNKS + 5
    vmem = pl.BlockSpec(memory_space=pltpu.VMEM)
    hbm = pl.BlockSpec(memory_space=pltpu.HBM)
    flops = 2 * 3 * taps * local_ch * channels * width
    block_out, input_grad, summed = pl.pallas_call(
        step_kernel,
        out_shape=(
            jax.ShapeDtypeStruct(inputs.shape, jnp.float32),
            jax.ShapeDtypeStruct(inputs.shape, jnp.float32),
            jax.ShapeDtypeStruct((all_rows, channels), jnp.bfloat16),
        ),
        in_specs=[hbm, vmem, hbm, hbm],
        out_specs=(vmem, vmem, vmem),
        scratch_shapes=[
            pltpu.VMEM((local_ch, width), jnp.float32),
            pltpu.VMEM((local_ch, width), jnp.float32),
            pltpu.VMEM((taps * local_ch, channels), jnp.float32),
            pltpu.VMEM((taps * local_ch, channels), jnp.bfloat16),
            pltpu.VMEM((channels, width), jnp.bfloat16),
            pltpu.VMEM((channels, width), jnp.bfloat16),
            pltpu.VMEM((local_ch, width), jnp.bfloat16),
            pltpu.VMEM((local_ch, width), jnp.bfloat16),
            pltpu.VMEM((all_rows, width), jnp.bfloat16),
            pltpu.VMEM((all_rows, width), jnp.bfloat16),
            pltpu.VMEM((local_ch, width), jnp.float32),
            pltpu.VMEM((local_ch, width), jnp.float32),
            pltpu.VMEM((channels, width), jnp.bfloat16),
            pltpu.VMEM((2, local_ch, width), jnp.bfloat16),
            pltpu.VMEM((local_ch, width), jnp.bfloat16),
            pltpu.VMEM((local_ch, width), jnp.bfloat16),
            pltpu.VMEM((CHUNKS, half, channels), jnp.float32),
            pltpu.VMEM((CHUNKS, half, channels), jnp.bfloat16),
            pltpu.VMEM((CHUNKS, DP_Z - 1, shard, channels), jnp.bfloat16),
            pltpu.SemaphoreType.DMA((3,)),
            pltpu.SemaphoreType.DMA((copies,)),
            pltpu.SemaphoreType.DMA((copies,)),
        ],
        compiler_params=pltpu.CompilerParams(
            collective_id=0, has_side_effects=True, vmem_limit_bytes=VMEM_STEP
        ),
        cost_estimate=pl.CostEstimate(
            flops=flops, bytes_accessed=8_000_000, transcendentals=4 * local_ch * width
        ),
    )(
        inputs,
        jnp.stack([norm_gain, norm_bias], axis=1),
        conv_weight.reshape(taps * local_ch, channels),
        out_grad,
    )
    flat = (taps * local_ch, channels)
    scale = 1.0 / (lax.axis_size("dp") * (width // (SIDE * SIDE)))
    block = pl.BlockSpec((local_ch, channels), lambda step: (step, 0))
    updated = pl.pallas_call(
        functools.partial(adam_kernel, scale),
        grid=(taps,),
        out_shape=(jax.ShapeDtypeStruct(flat, jnp.float32),) * 3,
        in_specs=[block] * 4,
        out_specs=(block,) * 3,
        cost_estimate=pl.CostEstimate(
            flops=16 * flat[0] * flat[1],
            bytes_accessed=26 * flat[0] * flat[1],
            transcendentals=2 * flat[0] * flat[1],
        ),
        compiler_params=pltpu.CompilerParams(vmem_limit_bytes=16 * 1024 * 1024),
    )(
        summed,
        conv_weight.reshape(flat),
        moment_one.reshape(flat),
        moment_two.reshape(flat),
    )
    weight_new, first_new, second_new = [leaf.reshape(conv_weight.shape) for leaf in updated]
    return (block_out, input_grad, weight_new, first_new, second_new)


def pick_body(inputs, *rest):
    fits = (
        lax.axis_size("dp") == DP_Y * DP_Z
        and lax.axis_size("fsdp") == FSDP
        and inputs.shape[1] == SIDE * SIDE
        and inputs.shape[0] % 16 == 0
    )
    return (fused_body if fits else body)(inputs, *rest)


def solution(mesh):
    placed = (
        P("fsdp", "dp"),
        P("fsdp"),
        P("fsdp"),
        P(None, "fsdp", None),
        P(None, "fsdp", None),
        P(None, "fsdp", None),
        P("fsdp", "dp"),
    )
    return jax.shard_map(
        pick_body,
        mesh=mesh,
        in_specs=placed,
        out_specs=(
            P("fsdp", "dp"),
            P("fsdp", "dp"),
            P(None, "fsdp", None),
            P(None, "fsdp", None),
            P(None, "fsdp", None),
        ),
        check_vma=False,
    )
```

```python
import functools

import jax
import jax.numpy as jnp
from jax import lax
from jax.experimental import pallas as pl
from jax.experimental.pallas import tpu as pltpu
from jax.sharding import PartitionSpec as P

GROUP_CH = 40
SIDE = 32


EPS_NORM = 1e-05
BETA_ONE = 0.9
BETA_TWO = 0.999
CORRECT_ONE = 1.0 - 0.9**10
CORRECT_TWO = 1.0 - 0.999**10
LEARN_RATE = 0.001
EPS_ADAM = 1e-08
OFFSETS = ((-1, -1), (-1, 0), (-1, 1), (0, -1), (0, 0), (0, 1), (1, -1), (1, 0), (1, 1))


def shifted(source, row_step, col_step):
    width_all = source.shape[-1]
    position = jnp.arange(width_all, dtype=jnp.int32)
    row_pos = position // SIDE % SIDE
    col_pos = position % SIDE
    inside = (
        (row_pos + row_step >= 0)
        & (row_pos + row_step < SIDE)
        & (col_pos + col_step >= 0)
        & (col_pos + col_step < SIDE)
    )
    margin = SIDE + 1
    padded = jnp.pad(source, ((0, 0), (margin, margin)))
    start_at = margin + row_step * SIDE + col_step
    moved = padded[:, start_at : start_at + width_all]
    return jnp.where(inside[None, :], moved, jnp.zeros_like(moved))


def group_stats(source, norm_gain, norm_bias):
    channels, width_all = source.shape
    images = width_all // (SIDE * SIDE)
    blocks = source.reshape(channels // GROUP_CH, GROUP_CH, images, SIDE * SIDE)
    mean_val = jnp.mean(blocks, axis=(1, 3), keepdims=True)
    centred = blocks - mean_val
    var_val = jnp.mean(centred * centred, axis=(1, 3), keepdims=True)
    inv_dev = lax.rsqrt(var_val + EPS_NORM)
    normed = (centred * inv_dev).reshape(channels, width_all)
    pre_act = normed * norm_gain[:, None] + norm_bias[:, None]
    return (normed, inv_dev, pre_act)


def group_backward(grad_act, pre_act, normed, inv_dev, norm_gain):
    channels, width_all = grad_act.shape
    images = width_all // (SIDE * SIDE)
    shape_four = (channels // GROUP_CH, GROUP_CH, images, SIDE * SIDE)
    sigmoid_val = jax.nn.sigmoid(pre_act)
    grad_pre = grad_act * sigmoid_val * (1.0 + pre_act * (1.0 - sigmoid_val))
    grad_norm = (grad_pre * norm_gain[:, None]).reshape(shape_four)
    normed_four = normed.reshape(shape_four)
    mean_first = jnp.mean(grad_norm, axis=(1, 3), keepdims=True)
    mean_second = jnp.mean(grad_norm * normed_four, axis=(1, 3), keepdims=True)
    return (inv_dev * (grad_norm - mean_first - normed_four * mean_second)).reshape(
        channels, width_all
    )


def body(inputs, norm_gain, norm_bias, conv_weight, moment_one, moment_two, out_grad):
    local_ch, group_width = inputs.shape
    images = group_width // (SIDE * SIDE)
    normed, inv_dev, pre_act = group_stats(inputs, norm_gain, norm_bias)
    activation = jax.nn.silu(pre_act).astype(jnp.bfloat16)
    weight_half = conv_weight.astype(jnp.bfloat16)
    grad_half = out_grad.astype(jnp.bfloat16)
    gathered = lax.all_gather(activation, "fsdp", axis=0, tiled=True)
    conv_out = jnp.zeros((local_ch, group_width), jnp.float32)
    grad_taps = []
    for tap_index, (row_step, col_step) in enumerate(OFFSETS):
        moved = shifted(gathered, row_step, col_step)
        conv_out = conv_out + jnp.dot(
            weight_half[tap_index], moved, preferred_element_type=jnp.float32
        )
        grad_taps.append(
            lax.dot_general(
                grad_half, moved, (((1,), (1,)), ((), ())), preferred_element_type=jnp.float32
            )
        )
    block_out = inputs + conv_out
    summed = lax.psum(jnp.stack(grad_taps), "dp")
    gradient = summed / (images * lax.axis_size("dp"))
    running = jnp.zeros((local_ch * lax.axis_size("fsdp"), group_width), jnp.float32)
    for tap_index, (row_step, col_step) in enumerate(OFFSETS):
        weight_part = weight_half[tap_index]
        back_term = lax.dot_general(
            weight_part, grad_half, (((0,), (0,)), ((), ())), preferred_element_type=jnp.float32
        )
        running = running + shifted(back_term, -row_step, -col_step)
    grad_act = lax.psum_scatter(running, "fsdp", scatter_dimension=0, tiled=True)
    input_grad = out_grad + group_backward(grad_act, pre_act, normed, inv_dev, norm_gain)
    first_new = BETA_ONE * moment_one + (1.0 - BETA_ONE) * gradient
    second_new = BETA_TWO * moment_two + (1.0 - BETA_TWO) * gradient * gradient
    weight_new = conv_weight - LEARN_RATE * (first_new / CORRECT_ONE) / (
        jnp.sqrt(second_new / CORRECT_TWO) + EPS_ADAM
    )
    return (block_out, input_grad, weight_new, first_new, second_new)


CHUNKS = 6
VMEM_STEP = 36 * 1024 * 1024
DP_Y = 2
DP_Z = 4
FSDP = 4
MESH = pl.DeviceIdType.MESH


def tap_mask(row_step, col_step):
    position = lax.broadcasted_iota(jnp.int32, (1, SIDE * SIDE), 1)
    row_pos = position // SIDE + row_step
    col_pos = position % SIDE + col_step
    inside = (row_pos >= 0) & (row_pos < SIDE) & (col_pos >= 0) & (col_pos < SIDE)
    return inside


def lane_shift(value, row_step, col_step):
    step = row_step * SIDE + col_step
    if step == 0:
        return value
    moved = pltpu.roll(value, (-step) % (SIDE * SIDE), 1)
    return jnp.where(tap_mask(row_step, col_step), moved, 0.0)


def step_kernel(
    x_ref,
    gain_ref,
    bias_ref,
    w_ref,
    g_ref,
    block_ref,
    igrad_ref,
    out_ref,
    w_full,
    w_half,
    act,
    shifted_g,
    normed_ref,
    pre_ref,
    back,
    from_sib,
    to_x,
    from_x,
    own_full,
    part,
    from_y,
    half_full,
    half_sum,
    from_z,
    w_sem,
    send_sem,
    recv_sem,
):
    local_ch, width = x_ref.shape
    taps = len(OFFSETS)
    all_rows = part.shape[0]
    chunk = all_rows // CHUNKS
    half = chunk // DP_Y
    shard = half // DP_Z
    dp, fs = lax.axis_index("dp"), lax.axis_index("fsdp")
    pos_z, pos_y = dp // DP_Y, dp % DP_Y
    sib = fs // 2 * 2 + (1 - fs % 2)
    far = (fs + 2) % FSDP
    far_sib = (sib + 2) % FSDP
    sib_id, far_id = (dp, sib), (dp, far)
    y_id = (pos_z * DP_Y + (1 - pos_y), fs)
    z_ids = [((pos_z + d) % DP_Z * DP_Y + pos_y, fs) for d in range(1, DP_Z)]
    next_z = pos_z // 2 * 2 + (1 - pos_z % 2)
    next_id, skip_id = (next_z * DP_Y + pos_y, fs), z_ids[1]

    w_copy = pltpu.make_async_copy(w_ref, w_full, w_sem)
    w_copy.start()
    barrier = pltpu.get_barrier_semaphore()
    peers = [sib_id, far_id, y_id] + z_ids
    for peer in peers:
        pl.semaphore_signal(barrier, inc=1, device_id=peer, device_id_type=MESH)

    def rows_of(index):
        return pl.ds(pl.multiple_of(index * local_ch, local_ch), local_ch)

    def remote(source, target, index, peer):
        return pltpu.make_async_remote_copy(
            src_ref=source,
            dst_ref=target,
            send_sem=send_sem.at[index],
            recv_sem=recv_sem.at[index],
            device_id=peer,
            device_id_type=MESH,
        )

    mine = rows_of(fs)
    inv_devs = []
    count = 1.0 / (GROUP_CH * width)
    pieces = []
    for group in range(local_ch // GROUP_CH):
        rows = slice(group * GROUP_CH, (group + 1) * GROUP_CH)
        value = x_ref[rows, :]
        mean_val = jnp.sum(value) * count
        centred = value - mean_val
        var_val = jnp.sum(centred * centred) * count
        inv_dev = lax.rsqrt(jnp.full((1, 1), var_val + EPS_NORM, jnp.float32))
        inv_devs.append(inv_dev)
        normed = centred * inv_dev
        pre_act = normed * gain_ref[rows, :] + bias_ref[rows, :]
        normed_ref[rows, :] = normed
        pre_ref[rows, :] = pre_act
        pieces.append(pre_act * jax.nn.sigmoid(pre_act))
    act[mine, :] = jnp.concatenate(pieces, axis=0).astype(jnp.bfloat16)

    pl.semaphore_wait(barrier, len(peers))
    act_sib = remote(act.at[mine], act.at[mine], 0, sib_id)
    act_far = remote(act.at[mine], act.at[mine], 1, far_id)
    act_far.start()
    act_sib.start()

    for tap, (row_step, col_step) in enumerate(OFFSETS):
        shifted_g[tap * local_ch : (tap + 1) * local_ch, :] = lane_shift(
            g_ref[...], -row_step, -col_step
        ).astype(jnp.bfloat16)
    spare = all_rows - taps * local_ch
    shifted_g[taps * local_ch :, :] = jnp.zeros((spare, width), jnp.bfloat16)

    tile = 512

    def back_tile(step):
        columns = slice(step * tile, (step + 1) * tile)
        back[:, columns] = lax.dot_general(
            w_half[...],
            shifted_g[: taps * local_ch, columns],
            (((0,), (0,)), ((), ())),
            preferred_element_type=jnp.float32,
        ).astype(jnp.bfloat16)

    back_far = remote(back.at[rows_of(far_sib)], from_sib.at[1], 4, sib_id)
    back_own = remote(back.at[rows_of(sib)], from_sib.at[0], 3, sib_id)

    act_far.wait_recv()
    act_forward = remote(act.at[rows_of(far)], act.at[rows_of(far)], 2, sib_id)
    act_forward.start()
    act_sib.wait_recv()
    act_forward.wait_recv()

    y_copies, z_copies, skip_copies, next_copies, yg_copies = [], [], [], [], []

    def half_rows(step, index):
        return pl.ds(pl.multiple_of(step * chunk + index * half, half), half)

    def partial_sums(first, last):
        rows = slice(first * chunk, last * chunk)
        product = lax.dot_general(
            shifted_g[rows, :],
            act[...],
            (((1,), (1,)), ((), ())),
            preferred_element_type=jnp.float32,
        )
        own_full[rows, :] = product
        part[rows, :] = product.astype(jnp.bfloat16)
        for step in range(first, last):
            sent = part.at[half_rows(step, 1 - pos_y)]
            copy = remote(sent, from_y.at[step], 6 + 8 * step, y_id)
            copy.start()
            y_copies.append(copy)

    def place(index_z):
        return index_z % 2 * 2 + index_z // 2

    def shard_rows(index_z):
        return pl.ds(pl.multiple_of(place(index_z) * shard, shard), shard)

    def sum_pair(step):
        y_copies[step].wait_recv()
        total = own_full[half_rows(step, pos_y), :] + from_y[step].astype(jnp.float32)
        half_full[step] = total
        half_sum[step] = total.astype(jnp.bfloat16)
        copies = []
        for d in (2, 1, 3):
            copy = remote(
                half_sum.at[step, shard_rows((pos_z + d) % DP_Z)],
                from_z.at[step, d - 1],
                6 + 8 * step + d,
                z_ids[d - 1],
            )
            copy.start()
            copies.append(copy)
        z_copies.append(copies)

    def sum_line(step):
        for copy in z_copies[step]:
            copy.wait_recv()
        total = half_full[step, shard_rows(pos_z), :]
        for d in range(DP_Z - 1):
            total = total + from_z[step, d].astype(jnp.float32)
        start = step * chunk + pos_y * half + place(pos_z) * shard
        rows = pl.ds(pl.multiple_of(start, shard), shard)
        out_ref[rows, :] = total.astype(jnp.bfloat16)
        copy = remote(out_ref.at[rows], out_ref.at[rows], 6 + 8 * step + 4, skip_id)
        copy.start()
        skip_copies.append(copy)

    def share_pair(step):
        skip_copies[step].wait_recv()
        start = step * chunk + pos_y * half + pos_z % 2 * 2 * shard
        rows = pl.ds(pl.multiple_of(start, 2 * shard), 2 * shard)
        copy = remote(out_ref.at[rows], out_ref.at[rows], 6 + 8 * step + 5, next_id)
        copy.start()
        next_copies.append(copy)

    def share_half(step):
        next_copies[step].wait_recv()
        rows = half_rows(step, pos_y)
        copy = remote(out_ref.at[rows], out_ref.at[rows], 6 + 8 * step + 7, y_id)
        copy.start()
        yg_copies.append(copy)

    def conv_taps(first, last):
        total = x_ref[...] if first == 0 else block_ref[...]
        product = jnp.dot(
            w_half[first * local_ch : last * local_ch, :],
            act[...],
            preferred_element_type=jnp.float32,
        )
        for tap in range(first, last):
            rows = slice((tap - first) * local_ch, (tap - first + 1) * local_ch)
            total = total + lane_shift(product[rows], *OFFSETS[tap])
        block_ref[...] = total

    partial_sums(0, 2)
    partial_sums(2, 4)
    sum_pair(0)
    partial_sums(4, 6)
    sum_pair(1)
    w_copy.wait()
    w_half[...] = w_full[...].astype(jnp.bfloat16)
    back_tile(0)
    sum_pair(2)
    sum_line(0)
    back_tile(1)
    back_far.start()
    back_own.start()
    sum_pair(3)
    sum_line(1)
    share_pair(0)
    conv_taps(0, 3)
    sum_pair(4)
    sum_line(2)
    share_pair(1)
    share_half(0)
    back_far.wait_recv()
    to_x[...] = (
        back[rows_of(far), :].astype(jnp.float32) + from_sib[1].astype(jnp.float32)
    ).astype(jnp.bfloat16)
    back_x = remote(to_x, from_x, 5, far_id)
    back_x.start()
    conv_taps(3, 6)
    sum_pair(5)
    sum_line(3)
    share_pair(2)
    share_half(1)
    conv_taps(6, 9)
    sum_line(4)
    share_pair(3)
    share_half(2)

    back_own.wait_recv()
    back_x.wait_recv()
    for group in range(local_ch // GROUP_CH):
        rows = slice(group * GROUP_CH, (group + 1) * GROUP_CH)
        grad_act = (
            back[mine, :].astype(jnp.float32)[rows]
            + from_sib[0].astype(jnp.float32)[rows]
            + from_x[...].astype(jnp.float32)[rows]
        )
        pre_act, normed = pre_ref[rows, :], normed_ref[rows, :]
        sigmoid_val = jax.nn.sigmoid(pre_act)
        grad_pre = grad_act * sigmoid_val * (1.0 + pre_act * (1.0 - sigmoid_val))
        grad_norm = grad_pre * gain_ref[rows, :]
        mean_first = jnp.sum(grad_norm) * count
        mean_second = jnp.sum(grad_norm * normed) * count
        igrad_ref[rows, :] = g_ref[rows, :] + inv_devs[group] * (
            grad_norm - mean_first - normed * mean_second
        )

    sum_line(5)
    share_pair(4)
    share_half(3)
    share_pair(5)
    share_half(4)
    share_half(5)
    for copy in yg_copies:
        copy.wait_recv()
    for copy in [act_sib, act_far, act_forward, back_far, back_own, back_x]:
        copy.wait_send()
    for copies in z_copies + [skip_copies, next_copies, y_copies, yg_copies]:
        for copy in copies:
            copy.wait_send()


def adam_kernel(scale, sum_ref, w_ref, one_ref, two_ref, w_out, one_out, two_out):
    gradient = sum_ref[...].astype(jnp.float32) * scale
    first_new = BETA_ONE * one_ref[...] + (1.0 - BETA_ONE) * gradient
    second_new = BETA_TWO * two_ref[...] + (1.0 - BETA_TWO) * gradient * gradient
    one_out[...] = first_new
    two_out[...] = second_new
    w_out[...] = w_ref[...] - LEARN_RATE * (first_new / CORRECT_ONE) / (
        jnp.sqrt(second_new / CORRECT_TWO) + EPS_ADAM
    )


def fused_body(inputs, norm_gain, norm_bias, conv_weight, moment_one, moment_two, out_grad):
    local_ch, width = inputs.shape
    taps, _, channels = conv_weight.shape
    unit = 16 * DP_Y * DP_Z * CHUNKS
    all_rows = (taps * local_ch + unit - 1) // unit * unit
    half = all_rows // CHUNKS // DP_Y
    shard = half // DP_Z
    copies = 6 + 8 * CHUNKS
    vmem = pl.BlockSpec(memory_space=pltpu.VMEM)
    flops = 2 * 3 * taps * local_ch * channels * width
    block_out, input_grad, summed = pl.pallas_call(
        step_kernel,
        out_shape=(
            jax.ShapeDtypeStruct(inputs.shape, jnp.float32),
            jax.ShapeDtypeStruct(inputs.shape, jnp.float32),
            jax.ShapeDtypeStruct((all_rows, channels), jnp.bfloat16),
        ),
        in_specs=[vmem, vmem, vmem, pl.BlockSpec(memory_space=pl.ANY), vmem],
        out_specs=(vmem, vmem, vmem),
        scratch_shapes=[
            pltpu.VMEM((taps * local_ch, channels), jnp.float32),
            pltpu.VMEM((taps * local_ch, channels), jnp.bfloat16),
            pltpu.VMEM((channels, width), jnp.bfloat16),
            pltpu.VMEM((all_rows, width), jnp.bfloat16),
            pltpu.VMEM((local_ch, width), jnp.float32),
            pltpu.VMEM((local_ch, width), jnp.float32),
            pltpu.VMEM((channels, width), jnp.bfloat16),
            pltpu.VMEM((2, local_ch, width), jnp.bfloat16),
            pltpu.VMEM((local_ch, width), jnp.bfloat16),
            pltpu.VMEM((local_ch, width), jnp.bfloat16),
            pltpu.VMEM((all_rows, channels), jnp.float32),
            pltpu.VMEM((all_rows, channels), jnp.bfloat16),
            pltpu.VMEM((CHUNKS, half, channels), jnp.bfloat16),
            pltpu.VMEM((CHUNKS, half, channels), jnp.float32),
            pltpu.VMEM((CHUNKS, half, channels), jnp.bfloat16),
            pltpu.VMEM((CHUNKS, DP_Z - 1, shard, channels), jnp.bfloat16),
            pltpu.SemaphoreType.DMA,
            pltpu.SemaphoreType.DMA((copies,)),
            pltpu.SemaphoreType.DMA((copies,)),
        ],
        compiler_params=pltpu.CompilerParams(
            collective_id=0, has_side_effects=True, vmem_limit_bytes=VMEM_STEP
        ),
        cost_estimate=pl.CostEstimate(
            flops=flops, bytes_accessed=8_000_000, transcendentals=4 * local_ch * width
        ),
    )(
        inputs,
        norm_gain[:, None],
        norm_bias[:, None],
        conv_weight.reshape(taps * local_ch, channels),
        out_grad,
    )
    flat = (taps * local_ch, channels)
    scale = 1.0 / (lax.axis_size("dp") * (width // (SIDE * SIDE)))
    block = pl.BlockSpec((local_ch, channels), lambda step: (step, 0))
    updated = pl.pallas_call(
        functools.partial(adam_kernel, scale),
        grid=(taps,),
        out_shape=(jax.ShapeDtypeStruct(flat, jnp.float32),) * 3,
        in_specs=[block] * 4,
        out_specs=(block,) * 3,
        cost_estimate=pl.CostEstimate(
            flops=16 * flat[0] * flat[1],
            bytes_accessed=26 * flat[0] * flat[1],
            transcendentals=2 * flat[0] * flat[1],
        ),
        compiler_params=pltpu.CompilerParams(vmem_limit_bytes=16 * 1024 * 1024),
    )(
        summed,
        conv_weight.reshape(flat),
        moment_one.reshape(flat),
        moment_two.reshape(flat),
    )
    weight_new, first_new, second_new = [leaf.reshape(conv_weight.shape) for leaf in updated]
    return (block_out, input_grad, weight_new, first_new, second_new)


def pick_body(inputs, *rest):
    fits = (
        lax.axis_size("dp") == DP_Y * DP_Z
        and lax.axis_size("fsdp") == FSDP
        and inputs.shape[1] == SIDE * SIDE
        and inputs.shape[0] % 16 == 0
    )
    return (fused_body if fits else body)(inputs, *rest)


def solution(mesh):
    placed = (
        P("fsdp", "dp"),
        P("fsdp"),
        P("fsdp"),
        P(None, "fsdp", None),
        P(None, "fsdp", None),
        P(None, "fsdp", None),
        P("fsdp", "dp"),
    )
    return jax.shard_map(
        pick_body,
        mesh=mesh,
        in_specs=placed,
        out_specs=(
            P("fsdp", "dp"),
            P("fsdp", "dp"),
            P(None, "fsdp", None),
            P(None, "fsdp", None),
            P(None, "fsdp", None),
        ),
        check_vma=False,
    )
```
